32 devices in a mesh: hyp: 2 (over x), row: 4 (over z), col: 4 (over y, core).
Axes of the slice: x: 2, y: 2, z: 4, core: 2. Of those that a mesh axis runs over, the one named last changes fastest.
Arguments:
- sigma_root: bfloat16 [16384, 8192], P(('hyp', 'row'), 'col'), parts along dimension 0, as said below
- lower1: bfloat16 [16384, 2048], P(('hyp', 'row'), 'col'), parts along dimension 0, may hold values from -0.125 to 0.125
- mask1: int32 [32, 8], replicated, may hold values 0 or 1
- inv1: bfloat16 [16, 256, 256], P(('hyp', 'col')), parts along dimension 0
- lower2: bfloat16 [16384, 1024], P(('hyp', 'row'), 'col'), parts along dimension 0, may hold values from -0.125 to 0.125
- mask2: int32 [32, 4], replicated, may hold values 0 or 1
- link2: bfloat16 [8, 256, 256], P(('hyp', 'col')), parts along dimension 0, may hold values from -0.375 to 0.375
- inv2: bfloat16 [8, 256, 256], P(('hyp', 'col')), parts along dimension 0
- parent: int32 [4], replicated, may hold values from 0 to 7, as said below
Outputs:
- off1: bfloat16 [16384, 2048], P(('hyp', 'row'), 'col'), parts along dimension 0
- diag1: bfloat16 [16, 256, 256], P(('hyp', 'col')), parts along dimension 0
- off2: bfloat16 [16384, 1024], P(('hyp', 'row'), 'col'), parts along dimension 0
- par2: bfloat16 [8, 256, 256], P(('hyp', 'col')), parts along dimension 0
- diag2: bfloat16 [8, 256, 256], P(('hyp', 'col')), parts along dimension 0
The draws below stay inside these ranges and needn't reach their ends.
There are 2 independent parts, one for each index of `hyp`. The reference program is written for one: setup_inputs(seed, part) draws one part's arguments, and reference() takes and returns one part's arrays. A program takes and returns all parts, laid end to end along the dimension named above; an argument that names none is the same for every part. Nothing has to cross between parts.
Inputs may be any that keep to these rules, and one draw needn't show every extreme that they name: `mask1`: 1 where block row i of the root lies in the structure of supernode p. `mask2`: 1 where block row i of the root lies in the structure of supernode k. The parent of supernode k lies in 2 * (k) to 2 * (k) + 1. `sigma_root`: symmetric.
All inputs are finite; a program needn't handle non-finite values.
Results may differ from the reference program's by a relative error of at most 0.0061.
Values may be sent and summed in bfloat16 or wider, within the bound.
A program may use at most 128 MiB of HBM per device.

```python
import math
import jax
import jax.numpy as jnp
from jax import lax

B = 256
NR = 32
P1C = 2
P2C = 1
P1 = 8
P2 = 4


def triangle(off, diagonal):
    size = off.shape[-1]
    row_ids = lax.broadcasted_iota(jnp.int32, (size, size), 0)
    col_ids = lax.broadcasted_iota(jnp.int32, (size, size), 1)
    below = (row_ids > col_ids).astype(jnp.float32)
    unit = (row_ids == col_ids).astype(jnp.float32)
    return off * below + diagonal[:, :, None] * unit


def draw_sigma_root(key, part):
    key = jax.random.fold_in(key, 11)
    first, second = jax.random.split(key, 2)
    total = NR * B
    raw = jax.random.normal(first, (total, total), jnp.float32) * (0.4 / math.sqrt(total))
    sym = (raw + raw.T) * 0.7071
    diagonal = jax.random.uniform(second, (total,), jnp.float32, 0.6, 1.8)
    ids = jnp.arange(total)
    result = sym + jnp.where(ids[:, None] == ids[None, :], diagonal[:, None], 0.0)
    return result.astype(jnp.bfloat16)


def draw_inv1(key, part):
    key = jax.random.fold_in(key, 21)
    first, second = jax.random.split(key)
    off = jax.random.normal(first, (P1, B, B), jnp.float32) * (0.5 / math.sqrt(B))
    diagonal = jax.random.uniform(second, (P1, B), jnp.float32, 0.6, 1.4)
    return triangle(off, diagonal).astype(jnp.bfloat16)


def draw_inv2(key, part):
    key = jax.random.fold_in(key, 31)
    first, second = jax.random.split(key)
    off = jax.random.normal(first, (P2, B, B), jnp.float32) * (0.5 / math.sqrt(B))
    diagonal = jax.random.uniform(second, (P2, B), jnp.float32, 0.6, 1.4)
    return triangle(off, diagonal).astype(jnp.bfloat16)


def draw_parent(key, part):
    key = jax.random.fold_in(key, 41)
    second = jax.random.fold_in(key, 1)
    wide = jax.random.randint(second, (P2,), 0, P1C * 7)
    offsets = wide % P1C
    ids = jnp.arange(P2, dtype=jnp.int32)
    chosen = ids // P2C * P1C + offsets
    chosen = jnp.where(ids == 0, 0, chosen)
    chosen = jnp.where(ids == P2 - 1, P1 - 1, chosen)
    return chosen.astype(jnp.int32)


def with_ends(values, key, least, largest):
    longest = values.shape.index(max(values.shape))
    spots = []
    for shift in (0, 1):
        where = [jax.random.randint(jax.random.fold_in(key, axis), (), 0, length) for axis, length in enumerate(values.shape)]
        where[longest] = (where[longest] + shift) % values.shape[longest]
        spots.append(tuple(where))
    return values.at[spots[0]].set(least).at[spots[1]].set(largest)


def block_scale(own_key, extent, pieces, low, top_value):
    factor_of, own = 1.0, jax.random.fold_in(own_key, 6)
    for dim, parts in pieces:
        steps = jnp.exp(jax.random.uniform(jax.random.fold_in(own, dim), (parts,), jnp.float32, low / len(pieces), top_value / len(pieces)))
        factor_of = factor_of * jnp.repeat(steps, extent[dim] // parts).reshape([-1 if axis == dim else 1 for axis in range(len(extent))])
    return factor_of


def scatter_about(own_key, shape, width, reach, cuts=(), kind=jnp.bfloat16):
    drawn = width * jax.random.normal(own_key, shape, jnp.float32)
    if cuts:
        drawn = drawn * block_scale(own_key, shape, cuts, -0.22, 0.18)
    return jnp.clip(drawn, -reach, reach).astype(kind)


def setup_inputs(seed: int = 0, part: int = 0) -> dict:
    splits = jax.random.split(jax.random.key(seed), 10)
    part_splits = jax.random.split(jax.random.fold_in(splits[9], part), 10)
    return {
        "sigma_root": draw_sigma_root(jax.random.fold_in(jax.random.fold_in(splits[9], part), 71), part),
        "lower1": scatter_about(part_splits[1], (NR * B, P1 * B), (NR * B // 4) ** -0.5, 0.125, ((0, 4), (1, 4))),
        "mask1": with_ends((jax.random.randint(splits[2], (NR, P1), 0, 3) < 2).astype(jnp.int32), jax.random.fold_in(splits[2], 1), 0, 1),
        "inv1": draw_inv1(jax.random.fold_in(jax.random.fold_in(splits[9], part), 71), part),
        "lower2": scatter_about(part_splits[4], (NR * B, P2 * B), (NR * B // 4) ** -0.5, 0.125, ((0, 4), (1, 4))),
        "mask2": with_ends((jax.random.randint(splits[5], (NR, P2), 0, 3) < 2).astype(jnp.int32), jax.random.fold_in(splits[5], 1), 0, 1),
        "link2": scatter_about(part_splits[6], (P2, B, B), B ** -0.5, 0.375, ((0, 4),)),
        "inv2": draw_inv2(jax.random.fold_in(jax.random.fold_in(splits[9], part), 71), part),
        "parent": draw_parent(jax.random.fold_in(splits[9], 71), part),
    }


def make_panel(lower, mask, inverse):
    blocks, count = mask.shape
    size = inverse.shape[1]
    masked = lower.reshape(blocks, size, count, size) * mask.astype(jnp.bfloat16)[:, None, :, None]
    masked = masked.reshape(blocks * size, count, size)
    product = jnp.einsum("rpb,pbd->rpd", masked.astype(jnp.float32), inverse.astype(jnp.float32))
    return product.astype(jnp.bfloat16)


def gram(first, second):
    return jnp.einsum("pcb,pcd->pbd", first.astype(jnp.float32), second.astype(jnp.float32))


def reference(sigma_root, lower1, mask1, inv1, lower2, mask2, link2, inv2, parent):
    rows = NR * B
    panel1 = make_panel(lower1, mask1, inv1)
    x_one = jnp.dot(sigma_root, panel1.reshape(rows, P1 * B), preferred_element_type=jnp.float32)
    off1 = (-x_one).astype(jnp.bfloat16)
    off1_blocks = off1.reshape(rows, P1, B)
    term1 = jnp.einsum("rpb,rpd->pbd", panel1.astype(jnp.float32), off1_blocks.astype(jnp.float32))
    diag1 = (gram(inv1, inv1) - term1).astype(jnp.bfloat16)
    panel2 = make_panel(lower2, mask2, inv2)
    link_u = jnp.einsum("kbc,kcd->kbd", link2.astype(jnp.float32), inv2.astype(jnp.float32)).astype(jnp.bfloat16)
    par_off = off1_blocks[:, parent, :]
    par_diag = diag1[parent]
    x_two = jnp.dot(sigma_root, panel2.reshape(rows, P2 * B), preferred_element_type=jnp.float32)
    extra = jnp.einsum("rkb,kbd->rkd", par_off.astype(jnp.float32), link_u.astype(jnp.float32))
    y_root = x_two + extra.reshape(rows, P2 * B)
    off2 = (-y_root).astype(jnp.bfloat16)
    cross = jnp.einsum("rkb,rkd->kbd", par_off.astype(jnp.float32), panel2.astype(jnp.float32))
    y_par = cross + jnp.einsum("kbc,kcd->kbd", par_diag.astype(jnp.float32), link_u.astype(jnp.float32))
    par2 = (-y_par).astype(jnp.bfloat16)
    pair = jnp.einsum("rkb,rkd->kbd", panel2.astype(jnp.float32), off2.reshape(rows, P2, B).astype(jnp.float32))
    diag2 = (gram(inv2, inv2) - pair - gram(link_u, par2)).astype(jnp.bfloat16)
    return off1, diag1, off2, par2, diag2
```

```python
import jax
import jax.numpy as jnp
from jax import lax
from jax.sharding import PartitionSpec as P


def per_device(sigma_root, lower1, mask1, inv1, lower2, mask2, link2, inv2, parent):
    block = inv1.shape[1]
    rows = sigma_root.shape[0]
    row_blocks = rows // block
    count1 = inv1.shape[0]
    count2 = inv2.shape[0]
    row_id = lax.axis_index("row")
    col_id = lax.axis_index("col")

    def make_panel(lower, mask, inverse):
        count = inverse.shape[0]
        window = lax.dynamic_slice(mask, (row_id * row_blocks, col_id * count), (row_blocks, count))
        masked = (
            lower.reshape(row_blocks, block, count, block)
            * window.astype(jnp.bfloat16)[:, None, :, None]
        )
        masked = masked.reshape(rows, count, block)
        product = jnp.einsum("rpb,pbd->rpd", masked, inverse, preferred_element_type=jnp.float32)
        return product.astype(jnp.bfloat16).reshape(rows, count * block)

    panel1 = make_panel(lower1, mask1, inv1)
    panel2 = make_panel(lower2, mask2, inv2)
    root_rows = lax.all_gather(sigma_root, "col", axis=1, tiled=True)

    def root_product(panel):
        return jnp.dot(
            root_rows,
            lax.all_gather(panel, "row", axis=0, tiled=True),
            preferred_element_type=jnp.float32,
        )

    x_one = root_product(panel1)
    x_two = root_product(panel2)
    off1 = (-x_one).astype(jnp.bfloat16)
    off1_blocks = off1.reshape(rows, count1, block)
    term1 = jnp.einsum(
        "rpb,rpd->pbd",
        panel1.reshape(rows, count1, block),
        off1_blocks,
        preferred_element_type=jnp.float32,
    )
    term1 = lax.psum(term1, "row")
    base1 = jnp.einsum("pcb,pcd->pbd", inv1, inv1, preferred_element_type=jnp.float32)
    diag1 = (base1 - term1).astype(jnp.bfloat16)
    link_u = jnp.einsum("kbc,kcd->kbd", link2, inv2, preferred_element_type=jnp.float32).astype(
        jnp.bfloat16
    )
    local_parent = lax.dynamic_slice_in_dim(parent, col_id * count2, count2) - col_id * count1
    pick = (local_parent[:, None] == jnp.arange(count1, dtype=jnp.int32)[None, :]).astype(
        jnp.bfloat16
    )
    par_off = jnp.einsum(
        "kp,rpb->rkb", pick, off1_blocks, preferred_element_type=jnp.float32
    ).astype(jnp.bfloat16)
    par_diag = jnp.einsum("kp,pbd->kbd", pick, diag1, preferred_element_type=jnp.float32).astype(
        jnp.bfloat16
    )
    panel2_blocks = panel2.reshape(rows, count2, block)
    extra = jnp.einsum("rkb,kbd->rkd", par_off, link_u, preferred_element_type=jnp.float32)
    y_root = x_two + extra.reshape(rows, count2 * block)
    off2 = (-y_root).astype(jnp.bfloat16)
    cross = jnp.einsum("rkb,rkd->kbd", par_off, panel2_blocks, preferred_element_type=jnp.float32)
    pair = jnp.einsum(
        "rkb,rkd->kbd",
        panel2_blocks,
        off2.reshape(rows, count2, block),
        preferred_element_type=jnp.float32,
    )
    cross, pair = lax.psum((cross, pair), "row")
    y_par = cross + jnp.einsum("kbc,kcd->kbd", par_diag, link_u, preferred_element_type=jnp.float32)
    par2 = (-y_par).astype(jnp.bfloat16)
    base2 = jnp.einsum("kcb,kcd->kbd", inv2, inv2, preferred_element_type=jnp.float32)
    last = jnp.einsum("kcb,kcd->kbd", link_u, par2, preferred_element_type=jnp.float32)
    diag2 = (base2 - pair - last).astype(jnp.bfloat16)
    return (off1, diag1, off2, par2, diag2)


def across(value, pairs):
    return lax.ppermute(value, ("row", "col"), pairs)


def place(side, step, core):
    row = step if side == 0 else 3 - step
    return 4 * row + 2 * side + core


def hops(edges):
    return [
        (place(side, a, core), place(side, b, core))
        for side in range(2)
        for core in range(2)
        for a, b in edges
    ]


def over(steps):
    return [
        (place(side, a, core), place(1 - side, 3 - a, core))
        for side in range(2)
        for core in range(2)
        for a in steps
    ]


def swap_cores():
    return [
        (place(side, a, core), place(side, a, 1 - core))
        for side in range(2)
        for core in range(2)
        for a in range(4)
    ]


def sum_rows(value):
    for flip in (1, 3):
        value = value + across(
            value, [(4 * r + c, 4 * (r ^ flip) + c) for r in range(4) for c in range(4)]
        )
    return value


def mul(a, b):
    return jnp.dot(a, b, preferred_element_type=jnp.float32)


def mul_t(a, b):
    return lax.dot_general(a, b, (((0,), (0,)), ((), ())), preferred_element_type=jnp.float32)


def per_device_chain(sigma_root, lower1, mask1, inv1, lower2, mask2, link2, inv2, parent):
    bf16 = jnp.bfloat16
    block = inv1.shape[1]
    rows = sigma_root.shape[0]
    row_blocks = rows // block
    count1 = inv1.shape[0]
    count2 = inv2.shape[0]
    row_id = lax.axis_index("row")
    col_id = lax.axis_index("col")
    side, core = col_id // 2, col_id % 2
    step = jnp.where(side == 0, row_id, 3 - row_id)
    first = core == side

    other = across(sigma_root, swap_cores())

    def panels(lower, mask, inverse):
        count = inverse.shape[0]
        window = lax.dynamic_slice(mask, (row_id * row_blocks, col_id * count), (row_blocks, count))
        out = []
        for p in range(count):
            piece = lower[:, p * block : (p + 1) * block].reshape(row_blocks, block, block)
            masked = (piece * window[:, p].astype(bf16)[:, None, None]).reshape(rows, block)
            out.append(mul(masked, inverse[p]).astype(bf16))
        return out

    def pick(a, b):
        return jnp.where(first, a, b)

    def root_product(v):
        r1 = across(v, hops([(0, 1), (1, 2)]))
        w = across(v, over([2, 3]))
        q_own = mul_t(sigma_root, v)
        d_own = across(q_own.astype(bf16), hops([(3, 2)]))
        q_other = mul_t(other, v)
        d_other = across(q_other.astype(bf16), hops([(3, 2)]))
        r2 = across(r1, hops([(1, 2), (2, 3)]))
        w_far = across(w, hops([(0, 1), (1, 0)]))
        s_own = across((q_own + d_own).astype(bf16), hops([(2, 1)]))
        s_other = across((q_other + d_other).astype(bf16), hops([(2, 1)]))
        r3 = across(r2, hops([(2, 3)]))
        w0 = jnp.where(step == 0, w, w_far)
        w1 = jnp.where(step == 0, w_far, w)
        g = mul(sigma_root, pick(w0, w1)) + mul(other, pick(w1, w0))
        g = across(g.astype(bf16), over([0, 1]))
        f0 = pick(s_own, s_other) + pick(q_own, q_other)
        f0 = across(f0.astype(bf16), hops([(1, 0)]))
        a = jnp.where(step == 0, v, jnp.where(step == 1, r1, jnp.where(step == 2, r2, r3)))
        b = jnp.where(step == 1, v, jnp.where(step == 2, r1, jnp.where(step == 3, r2, 0)))
        x = mul(sigma_root, pick(a, b)) + mul(other, pick(b, a))
        rest = jnp.where(step == 0, f0, jnp.where(step == 1, pick(s_other, s_own), g))
        return x + rest

    u1 = panels(lower1, mask1, inv1)
    u2 = panels(lower2, mask2, inv2)
    off1 = [(-root_product(u)).astype(bf16) for u in u1]
    term1 = sum_rows(jnp.stack([mul_t(u, o) for u, o in zip(u1, off1)]))
    base1 = jnp.stack([mul_t(inv1[p], inv1[p]) for p in range(count1)])
    diag1 = (base1 - term1).astype(bf16)
    off2, par2, diag2 = [], [], []
    for k in range(count2):
        which = lax.dynamic_index_in_dim(parent, col_id * count2 + k, keepdims=False)
        which = which - col_id * count1
        par_off, par_diag = off1[0], diag1[0]
        for p in range(1, count1):
            par_off = jnp.where(which == p, off1[p], par_off)
            par_diag = jnp.where(which == p, diag1[p], par_diag)
        link_u = mul(link2[k], inv2[k]).astype(bf16)
        cross = sum_rows(mul_t(par_off, u2[k]))
        par = (-(cross + mul(par_diag, link_u))).astype(bf16)
        known = mul_t(inv2[k], inv2[k]) - mul_t(link_u, par)
        o2 = (-(root_product(u2[k]) + mul(par_off, link_u))).astype(bf16)
        pair = sum_rows(mul_t(u2[k], o2))
        off2.append(o2)
        par2.append(par)
        diag2.append((known - pair).astype(bf16))
    return (
        jnp.concatenate(off1, axis=1),
        diag1,
        jnp.concatenate(off2, axis=1),
        jnp.stack(par2),
        jnp.stack(diag2),
    )


def solution(mesh):
    chain = mesh.shape["row"] == 4 and mesh.shape["col"] == 4
    body = per_device_chain if chain else per_device
    placed = (
        P(("hyp", "row"), "col"),
        P(("hyp", "row"), "col"),
        P(),
        P(("hyp", "col"), None, None),
        P(("hyp", "row"), "col"),
        P(),
        P(("hyp", "col"), None, None),
        P(("hyp", "col"), None, None),
        P(),
    )
    return jax.shard_map(
        body,
        mesh=mesh,
        in_specs=placed,
        out_specs=(
            P(("hyp", "row"), "col"),
            P(("hyp", "col"), None, None),
            P(("hyp", "row"), "col"),
            P(("hyp", "col"), None, None),
            P(("hyp", "col"), None, None),
        ),
        check_vma=False,
    )
```

```python
import jax
import jax.numpy as jnp
from jax import lax
from jax.sharding import PartitionSpec as P


def per_device(sigma_root, lower1, mask1, inv1, lower2, mask2, link2, inv2, parent):
    block = inv1.shape[1]
    rows = sigma_root.shape[0]
    row_blocks = rows // block
    count1 = inv1.shape[0]
    count2 = inv2.shape[0]
    row_id = lax.axis_index("row")
    col_id = lax.axis_index("col")

    def make_panel(lower, mask, inverse):
        count = inverse.shape[0]
        window = lax.dynamic_slice(mask, (row_id * row_blocks, col_id * count), (row_blocks, count))
        masked = (
            lower.reshape(row_blocks, block, count, block)
            * window.astype(jnp.bfloat16)[:, None, :, None]
        )
        masked = masked.reshape(rows, count, block)
        product = jnp.einsum("rpb,pbd->rpd", masked, inverse, preferred_element_type=jnp.float32)
        return product.astype(jnp.bfloat16).reshape(rows, count * block)

    panel1 = make_panel(lower1, mask1, inv1)
    panel2 = make_panel(lower2, mask2, inv2)
    root_rows = lax.all_gather(sigma_root, "col", axis=1, tiled=True)

    def root_product(panel):
        return jnp.dot(
            root_rows,
            lax.all_gather(panel, "row", axis=0, tiled=True),
            preferred_element_type=jnp.float32,
        )

    x_one = root_product(panel1)
    x_two = root_product(panel2)
    off1 = (-x_one).astype(jnp.bfloat16)
    off1_blocks = off1.reshape(rows, count1, block)
    term1 = jnp.einsum(
        "rpb,rpd->pbd",
        panel1.reshape(rows, count1, block),
        off1_blocks,
        preferred_element_type=jnp.float32,
    )
    term1 = lax.psum(term1, "row")
    base1 = jnp.einsum("pcb,pcd->pbd", inv1, inv1, preferred_element_type=jnp.float32)
    diag1 = (base1 - term1).astype(jnp.bfloat16)
    link_u = jnp.einsum("kbc,kcd->kbd", link2, inv2, preferred_element_type=jnp.float32).astype(
        jnp.bfloat16
    )
    local_parent = lax.dynamic_slice_in_dim(parent, col_id * count2, count2) - col_id * count1
    pick = (local_parent[:, None] == jnp.arange(count1, dtype=jnp.int32)[None, :]).astype(
        jnp.bfloat16
    )
    par_off = jnp.einsum(
        "kp,rpb->rkb", pick, off1_blocks, preferred_element_type=jnp.float32
    ).astype(jnp.bfloat16)
    par_diag = jnp.einsum("kp,pbd->kbd", pick, diag1, preferred_element_type=jnp.float32).astype(
        jnp.bfloat16
    )
    panel2_blocks = panel2.reshape(rows, count2, block)
    extra = jnp.einsum("rkb,kbd->rkd", par_off, link_u, preferred_element_type=jnp.float32)
    y_root = x_two + extra.reshape(rows, count2 * block)
    off2 = (-y_root).astype(jnp.bfloat16)
    cross = jnp.einsum("rkb,rkd->kbd", par_off, panel2_blocks, preferred_element_type=jnp.float32)
    pair = jnp.einsum(
        "rkb,rkd->kbd",
        panel2_blocks,
        off2.reshape(rows, count2, block),
        preferred_element_type=jnp.float32,
    )
    cross, pair = lax.psum((cross, pair), "row")
    y_par = cross + jnp.einsum("kbc,kcd->kbd", par_diag, link_u, preferred_element_type=jnp.float32)
    par2 = (-y_par).astype(jnp.bfloat16)
    base2 = jnp.einsum("kcb,kcd->kbd", inv2, inv2, preferred_element_type=jnp.float32)
    last = jnp.einsum("kcb,kcd->kbd", link_u, par2, preferred_element_type=jnp.float32)
    diag2 = (base2 - pair - last).astype(jnp.bfloat16)
    return (off1, diag1, off2, par2, diag2)


def across(value, pairs):
    return lax.ppermute(value, ("row", "col"), pairs)


def place(side, step, core):
    row = step if side == 0 else 3 - step
    return 4 * row + 2 * side + core


def hops(edges):
    return [
        (place(side, a, core), place(side, b, core))
        for side in range(2)
        for core in range(2)
        for a, b in edges
    ]


def over(steps):
    return [
        (place(side, a, core), place(1 - side, 3 - a, core))
        for side in range(2)
        for core in range(2)
        for a in steps
    ]


def swap_cores():
    return [
        (place(side, a, core), place(side, a, 1 - core))
        for side in range(2)
        for core in range(2)
        for a in range(4)
    ]


def sum_rows(value):
    for flip in (1, 3):
        value = value + across(
            value, [(4 * r + c, 4 * (r ^ flip) + c) for r in range(4) for c in range(4)]
        )
    return value


def mul(a, b):
    return jnp.dot(a, b, preferred_element_type=jnp.float32)


def mul_t(a, b):
    return lax.dot_general(a, b, (((0,), (0,)), ((), ())), preferred_element_type=jnp.float32)


def per_device_chain(sigma_root, lower1, mask1, inv1, lower2, mask2, link2, inv2, parent):
    bf16 = jnp.bfloat16
    block = inv1.shape[1]
    rows = sigma_root.shape[0]
    row_blocks = rows // block
    count1 = inv1.shape[0]
    count2 = inv2.shape[0]
    row_id = lax.axis_index("row")
    col_id = lax.axis_index("col")
    side, core = col_id // 2, col_id % 2
    step = jnp.where(side == 0, row_id, 3 - row_id)
    first = core == side

    other = across(sigma_root, swap_cores())

    def panels(lower, mask, inverse):
        count = inverse.shape[0]
        window = lax.dynamic_slice(mask, (row_id * row_blocks, col_id * count), (row_blocks, count))
        out = []
        for p in range(count):
            piece = lower[:, p * block : (p + 1) * block].reshape(row_blocks, block, block)
            masked = (piece * window[:, p].astype(bf16)[:, None, None]).reshape(rows, block)
            out.append(mul(masked, inverse[p]).astype(bf16))
        return out

    def pick(a, b):
        return jnp.where(first, a, b)

    def cut(wide, count):
        return [wide[:, p * block : (p + 1) * block] for p in range(count)]

    def wide(parts):
        return parts[0] if len(parts) == 1 else jnp.concatenate(parts, axis=1)

    def add(*parts):
        return sum(p.astype(jnp.float32) for p in parts)

    def root_products(v, groups):
        n = len(v)
        last = n - 1
        q_own = mul_t(sigma_root, wide(v)).astype(bf16)
        q_own = cut(q_own, n)
        r1 = [across(p, hops([(0, 1), (1, 2)])) for p in v]
        d_own = [across(p, hops([(3, 2)])) for p in q_own]
        w = [across(p, over([2, 3])) for p in v]
        held, r1[0] = lax.optimization_barrier((other, r1[0]))
        q_other = mul_t(held, wide(v)).astype(bf16)
        q_other, r1[last] = lax.optimization_barrier((q_other, r1[last]))
        q_other = cut(q_other, n)
        d_other = [across(p, hops([(3, 2)])) for p in q_other]
        s_own = [across(add(p, d).astype(bf16), hops([(2, 1)])) for p, d in zip(q_own, d_own)]
        r2 = [across(p, hops([(1, 2), (2, 3)])) for p in r1]
        w_far = [across(p, hops([(0, 1), (1, 0)])) for p in w]
        s_other = [across(add(p, d).astype(bf16), hops([(2, 1)])) for p, d in zip(q_other, d_other)]
        w0 = [jnp.where(step == 0, p, far) for p, far in zip(w, w_far)]
        w1 = [jnp.where(step == 0, far, p) for p, far in zip(w, w_far)]
        g = mul(sigma_root, wide([pick(p, q) for p, q in zip(w0, w1)]))
        g = (g + mul(held, wide([pick(q, p) for p, q in zip(w0, w1)]))).astype(bf16)
        g, r2[last] = lax.optimization_barrier((g, r2[last]))
        g = [across(p, over([0, 1])) for p in cut(g, n)]
        r3 = [across(p, hops([(2, 3)])) for p in r2]
        f0 = [
            across(add(pick(s_own[p], s_other[p]), pick(q_own[p], q_other[p])).astype(bf16), hops([(1, 0)]))
            for p in range(n)
        ]
        result, start = [], 0
        for size in groups:
            here = range(start, start + size)
            a, b, rest = [], [], []
            for p in here:
                x0 = jnp.where(step == 2, r2[p], r3[p])
                x0 = jnp.where(step == 0, v[p], jnp.where(step == 1, r1[p], x0))
                x1 = jnp.where(step == 2, r1[p], jnp.where(step == 3, r2[p], 0))
                x1 = jnp.where(step == 1, v[p], x1)
                a.append(pick(x0, x1))
                b.append(pick(x1, x0))
                late = jnp.where(step == 1, pick(s_other[p], s_own[p]), g[p])
                rest.append(jnp.where(step == 0, f0[p], late))
            result.append(mul(sigma_root, wide(a)) + mul(held, wide(b)) + wide(rest))
            start += size
        return result

    u1 = panels(lower1, mask1, inv1)
    u2 = panels(lower2, mask2, inv2)
    x1, x2 = root_products(u1 + u2, (count1, count2))
    off1_wide = (-x1).astype(bf16)
    off1 = cut(off1_wide, count1)
    x2 = cut(x2, count2)
    term1 = sum_rows(jnp.stack([mul_t(u, o) for u, o in zip(u1, off1)]))
    base1 = jnp.stack([mul_t(inv1[p], inv1[p]) for p in range(count1)])
    diag1 = (base1 - term1).astype(bf16)
    off2, par2, diag2 = [], [], []
    for k in range(count2):
        which = lax.dynamic_index_in_dim(parent, col_id * count2 + k, keepdims=False)
        which = which - col_id * count1
        par_off, par_diag = off1[0], diag1[0]
        for p in range(1, count1):
            par_off = jnp.where(which == p, off1[p], par_off)
            par_diag = jnp.where(which == p, diag1[p], par_diag)
        link_u = mul(link2[k], inv2[k]).astype(bf16)
        cross = sum_rows(mul_t(par_off, u2[k]))
        par = (-(cross + mul(par_diag, link_u))).astype(bf16)
        known = mul_t(inv2[k], inv2[k]) - mul_t(link_u, par)
        o2 = (-(x2[k] + mul(par_off, link_u))).astype(bf16)
        pair = sum_rows(mul_t(u2[k], o2))
        off2.append(o2)
        par2.append(par)
        diag2.append((known - pair).astype(bf16))
    return (
        off1_wide,
        diag1,
        jnp.concatenate(off2, axis=1),
        jnp.stack(par2),
        jnp.stack(diag2),
    )


def solution(mesh):
    chain = mesh.shape["row"] == 4 and mesh.shape["col"] == 4
    body = per_device_chain if chain else per_device
    placed = (
        P(("hyp", "row"), "col"),
        P(("hyp", "row"), "col"),
        P(),
        P(("hyp", "col"), None, None),
        P(("hyp", "row"), "col"),
        P(),
        P(("hyp", "col"), None, None),
        P(("hyp", "col"), None, None),
        P(),
    )
    return jax.shard_map(
        body,
        mesh=mesh,
        in_specs=placed,
        out_specs=(
            P(("hyp", "row"), "col"),
            P(("hyp", "col"), None, None),
            P(("hyp", "row"), "col"),
            P(("hyp", "col"), None, None),
            P(("hyp", "col"), None, None),
        ),
        check_vma=False,
    )
```

```python
import functools

import jax
import jax.numpy as jnp
from jax import lax
from jax.sharding import PartitionSpec as P


def sum_rows(value, size):
    if size != 4:
        return lax.psum(value, "row")
    for flip in (1, 3):
        value = value + lax.ppermute(value, "row", [(r, r ^ flip) for r in range(size)])
    return value


def gather_rows(panel, size):
    me = lax.axis_index("row")
    up, down, ups, downs = panel, panel, [], []
    for hop in range(1, size):
        up = lax.ppermute(up, "row", [(r, r + 1) for r in range(hop - 1, size - 1)])
        down = lax.ppermute(down, "row", [(r, r - 1) for r in range(1, size - hop + 1)])
        ups.append(up)
        downs.append(down)
    whole = jnp.zeros((size,) + panel.shape, panel.dtype)
    whole = lax.dynamic_update_index_in_dim(whole, panel, me, 0)
    for hop in range(1, size):
        block = jnp.where(me >= hop, ups[hop - 1], downs[size - hop - 1])
        whole = lax.dynamic_update_index_in_dim(whole, block, lax.rem(me - hop + size, size), 0)
    return whole.reshape(size * panel.shape[0], panel.shape[1])


def per_device(size, sigma_root, lower1, mask1, inv1, lower2, mask2, link2, inv2, parent):
    block = inv1.shape[1]
    rows = sigma_root.shape[0]
    row_blocks = rows // block
    count1 = inv1.shape[0]
    count2 = inv2.shape[0]
    row_id = lax.axis_index("row")
    col_id = lax.axis_index("col")

    def make_panel(lower, mask, inverse):
        count = inverse.shape[0]
        window = lax.dynamic_slice(mask, (row_id * row_blocks, col_id * count), (row_blocks, count))
        masked = (
            lower.reshape(row_blocks, block, count, block)
            * window.astype(jnp.bfloat16)[:, None, :, None]
        )
        masked = masked.reshape(rows, count, block)
        product = jnp.einsum("rpb,pbd->rpd", masked, inverse, preferred_element_type=jnp.float32)
        return product.astype(jnp.bfloat16).reshape(rows, count * block)

    panel1 = make_panel(lower1, mask1, inv1)
    panel2 = make_panel(lower2, mask2, inv2)
    root_rows = lax.all_gather(sigma_root, "col", axis=1, tiled=True)

    width = count1 * block
    everything = gather_rows(jnp.concatenate([panel1, panel2], axis=1), size)
    x_one = jnp.dot(root_rows, everything[:, :width], preferred_element_type=jnp.float32)
    x_two = jnp.dot(root_rows, everything[:, width:], preferred_element_type=jnp.float32)
    off1 = (-x_one).astype(jnp.bfloat16)
    off1_blocks = off1.reshape(rows, count1, block)
    term1 = jnp.einsum(
        "rpb,rpd->pbd",
        panel1.reshape(rows, count1, block),
        off1_blocks,
        preferred_element_type=jnp.float32,
    )
    term1 = sum_rows(term1, size)
    base1 = jnp.einsum("pcb,pcd->pbd", inv1, inv1, preferred_element_type=jnp.float32)
    diag1 = (base1 - term1).astype(jnp.bfloat16)
    link_u = jnp.einsum("kbc,kcd->kbd", link2, inv2, preferred_element_type=jnp.float32).astype(
        jnp.bfloat16
    )
    local_parent = lax.dynamic_slice_in_dim(parent, col_id * count2, count2) - col_id * count1
    pick = (local_parent[:, None] == jnp.arange(count1, dtype=jnp.int32)[None, :]).astype(
        jnp.bfloat16
    )
    par_off = jnp.einsum(
        "kp,rpb->rkb", pick, off1_blocks, preferred_element_type=jnp.float32
    ).astype(jnp.bfloat16)
    par_diag = jnp.einsum("kp,pbd->kbd", pick, diag1, preferred_element_type=jnp.float32).astype(
        jnp.bfloat16
    )
    panel2_blocks = panel2.reshape(rows, count2, block)
    extra = jnp.einsum("rkb,kbd->rkd", par_off, link_u, preferred_element_type=jnp.float32)
    y_root = x_two + extra.reshape(rows, count2 * block)
    off2 = (-y_root).astype(jnp.bfloat16)
    cross = jnp.einsum("rkb,rkd->kbd", par_off, panel2_blocks, preferred_element_type=jnp.float32)
    pair = jnp.einsum(
        "rkb,rkd->kbd",
        panel2_blocks,
        off2.reshape(rows, count2, block),
        preferred_element_type=jnp.float32,
    )
    cross, pair = sum_rows(cross, size), sum_rows(pair, size)
    y_par = cross + jnp.einsum("kbc,kcd->kbd", par_diag, link_u, preferred_element_type=jnp.float32)
    par2 = (-y_par).astype(jnp.bfloat16)
    base2 = jnp.einsum("kcb,kcd->kbd", inv2, inv2, preferred_element_type=jnp.float32)
    last = jnp.einsum("kcb,kcd->kbd", link_u, par2, preferred_element_type=jnp.float32)
    diag2 = (base2 - pair - last).astype(jnp.bfloat16)
    return (off1, diag1, off2, par2, diag2)


def solution(mesh):
    placed = (
        P(("hyp", "row"), "col"),
        P(("hyp", "row"), "col"),
        P(),
        P(("hyp", "col"), None, None),
        P(("hyp", "row"), "col"),
        P(),
        P(("hyp", "col"), None, None),
        P(("hyp", "col"), None, None),
        P(),
    )
    return jax.shard_map(
        functools.partial(per_device, mesh.shape["row"]),
        mesh=mesh,
        in_specs=placed,
        out_specs=(
            P(("hyp", "row"), "col"),
            P(("hyp", "col"), None, None),
            P(("hyp", "row"), "col"),
            P(("hyp", "col"), None, None),
            P(("hyp", "col"), None, None),
        ),
        check_vma=False,
    )
```

```python
import functools

import jax
import jax.numpy as jnp
from jax import lax
from jax.sharding import PartitionSpec as P


def exchange(value, flip):
    return value + lax.ppermute(value, "row", [(r, r ^ flip) for r in range(4)])


def sum_rows(value, size):
    if size != 4:
        return lax.psum(value, "row")
    return exchange(exchange(value, 1), 3)


def hop_rows(panel, size):
    up, down, ups, downs = panel, panel, [], []
    for hop in range(1, size):
        up = lax.ppermute(up, "row", [(r, r + 1) for r in range(hop - 1, size - 1)])
        down = lax.ppermute(down, "row", [(r, r - 1) for r in range(1, size - hop + 1)])
        ups.append(up)
        downs.append(down)
    return ups, downs


def collect_rows(panel, ups, downs, size):
    me = lax.axis_index("row")
    whole = jnp.zeros((size,) + panel.shape, panel.dtype)
    whole = lax.dynamic_update_index_in_dim(whole, panel, me, 0)
    for hop in range(1, size):
        block = jnp.where(me >= hop, ups[hop - 1], downs[size - hop - 1])
        whole = lax.dynamic_update_index_in_dim(whole, block, lax.rem(me - hop + size, size), 0)
    return whole.reshape(size * panel.shape[0], panel.shape[1])


def per_device(size, sigma_root, lower1, mask1, inv1, lower2, mask2, link2, inv2, parent):
    block = inv1.shape[1]
    rows = sigma_root.shape[0]
    row_blocks = rows // block
    count1 = inv1.shape[0]
    count2 = inv2.shape[0]
    row_id = lax.axis_index("row")
    col_id = lax.axis_index("col")

    def make_panel(lower, mask, inverse):
        count = inverse.shape[0]
        window = lax.dynamic_slice(mask, (row_id * row_blocks, col_id * count), (row_blocks, count))
        masked = (
            lower.reshape(row_blocks, block, count, block)
            * window.astype(jnp.bfloat16)[:, None, :, None]
        )
        masked = masked.reshape(rows, count, block)
        product = jnp.einsum("rpb,pbd->rpd", masked, inverse, preferred_element_type=jnp.float32)
        return product.astype(jnp.bfloat16).reshape(rows, count * block)

    panel1 = make_panel(lower1, mask1, inv1)
    panel2 = make_panel(lower2, mask2, inv2)
    root_rows = lax.all_gather(sigma_root, "col", axis=1, tiled=True)

    ups, downs = hop_rows(panel1, size)
    next_panel, ups[-1], downs[-1] = lax.optimization_barrier((panel2, ups[-1], downs[-1]))
    every1 = collect_rows(panel1, ups, downs, size)
    every2 = collect_rows(next_panel, *hop_rows(next_panel, size), size)
    x_one = jnp.dot(root_rows, every1, preferred_element_type=jnp.float32)
    off1 = (-x_one).astype(jnp.bfloat16)
    off1_blocks = off1.reshape(rows, count1, block)
    term1 = jnp.einsum(
        "rpb,rpd->pbd",
        panel1.reshape(rows, count1, block),
        off1_blocks,
        preferred_element_type=jnp.float32,
    )
    local_parent = lax.dynamic_slice_in_dim(parent, col_id * count2, count2) - col_id * count1
    pick = (local_parent[:, None] == jnp.arange(count1, dtype=jnp.int32)[None, :]).astype(
        jnp.bfloat16
    )
    par_off = jnp.einsum(
        "kp,rpb->rkb", pick, off1_blocks, preferred_element_type=jnp.float32
    ).astype(jnp.bfloat16)
    panel2_blocks = panel2.reshape(rows, count2, block)
    cross = jnp.einsum("rkb,rkd->kbd", par_off, panel2_blocks, preferred_element_type=jnp.float32)
    half = rows // 2
    terms = jnp.concatenate([term1, cross], axis=0)
    if size == 4:
        terms = exchange(terms, 1)
    top = jnp.dot(root_rows[:half], every2, preferred_element_type=jnp.float32)
    top, terms = lax.optimization_barrier((top, terms))
    terms = exchange(terms, 3) if size == 4 else lax.psum(terms, "row")
    bottom = jnp.dot(root_rows[half:], every2, preferred_element_type=jnp.float32)
    x_two = jnp.concatenate([top, bottom], axis=0)
    term1, cross = terms[:count1], terms[count1:]
    base1 = jnp.einsum("pcb,pcd->pbd", inv1, inv1, preferred_element_type=jnp.float32)
    diag1 = (base1 - term1).astype(jnp.bfloat16)
    link_u = jnp.einsum("kbc,kcd->kbd", link2, inv2, preferred_element_type=jnp.float32).astype(
        jnp.bfloat16
    )
    par_diag = jnp.einsum("kp,pbd->kbd", pick, diag1, preferred_element_type=jnp.float32).astype(
        jnp.bfloat16
    )
    extra = jnp.einsum("rkb,kbd->rkd", par_off, link_u, preferred_element_type=jnp.float32)
    y_root = x_two + extra.reshape(rows, count2 * block)
    off2 = (-y_root).astype(jnp.bfloat16)
    pair = jnp.einsum(
        "rkb,rkd->kbd",
        panel2_blocks,
        off2.reshape(rows, count2, block),
        preferred_element_type=jnp.float32,
    )
    pair = sum_rows(pair, size)
    y_par = cross + jnp.einsum("kbc,kcd->kbd", par_diag, link_u, preferred_element_type=jnp.float32)
    par2 = (-y_par).astype(jnp.bfloat16)
    base2 = jnp.einsum("kcb,kcd->kbd", inv2, inv2, preferred_element_type=jnp.float32)
    last = jnp.einsum("kcb,kcd->kbd", link_u, par2, preferred_element_type=jnp.float32)
    diag2 = (base2 - pair - last).astype(jnp.bfloat16)
    return (off1, diag1, off2, par2, diag2)


def solution(mesh):
    placed = (
        P(("hyp", "row"), "col"),
        P(("hyp", "row"), "col"),
        P(),
        P(("hyp", "col"), None, None),
        P(("hyp", "row"), "col"),
        P(),
        P(("hyp", "col"), None, None),
        P(("hyp", "col"), None, None),
        P(),
    )
    return jax.shard_map(
        functools.partial(per_device, mesh.shape["row"]),
        mesh=mesh,
        in_specs=placed,
        out_specs=(
            P(("hyp", "row"), "col"),
            P(("hyp", "col"), None, None),
            P(("hyp", "row"), "col"),
            P(("hyp", "col"), None, None),
            P(("hyp", "col"), None, None),
        ),
        check_vma=False,
    )
```
